32 devices in a mesh: groups: 1, expert: 16 (over z, y, x), dp: 2 (over core).
Axes of the slice: x: 2, y: 2, z: 4, core: 2. Of those that a mesh axis runs over, the one named last changes fastest.
Arguments:
- tokens: bfloat16 [2048, 3584], P(('groups', 'expert', 'dp')), may hold values from -6 to 6
- router_logits: float32 [2048, 8], P(('groups', 'expert', 'dp')), may hold values from -6 to 6
- expert_ids: int32 [2048, 8], P(('groups', 'expert', 'dp')), may hold values from 0 to 15, all different within a row; in each aligned block of 64 rows (0 to 63, 64 to 127, ...) at most 40 rows name the same one
- gate_up: bfloat16 [16, 2, 3584, 1024], P('expert', None, None, 'dp'), may hold values from -0.09375 to 0.09375
- down_proj: bfloat16 [16, 1024, 3584], P('expert', 'dp'), may hold values from -0.1875 to 0.1875
- latent_cache: bfloat16 [32, 512, 576], P(('groups', 'expert', 'dp')), may hold values from -4 to 4
- cache_len: int32 [32], P(('groups', 'expert', 'dp')), may hold values from 128 to 510, as said below
- new_latent: bfloat16 [32, 2, 576], P(('groups', 'expert', 'dp')), may hold values from -4 to 4
- queries: bfloat16 [32, 2, 128, 576], P(('groups', 'expert', 'dp')), may hold values from -28 to 28
Outputs:
- mixed_tokens: bfloat16 [2048, 3584], P(('groups', 'expert', 'dp'))
- context: bfloat16 [32, 2, 128, 512], P(('groups', 'expert', 'dp'))
The draws below stay inside these ranges and needn't reach their ends.
Inputs may be any that keep to these rules, and one draw needn't show every extreme that they name: `expert_ids`: each token names 8 different experts; among the 64 tokens of one device no expert is named by more than 40 tokens, a bound that some block reaches. `cache_len`: some request has exactly 510 live rows and some exactly 128.
All inputs are finite; a program needn't handle non-finite values.
Results may differ from the reference program's by a relative error of at most 0.008.
Values may be sent and summed in bfloat16 or wider, within the bound.
A program may use at most 128 MiB of HBM per device.

```python
import math
import jax
import jax.numpy as jnp
import numpy as np
from jax import lax

D = 3584
FF = 1024
HEADS = 128
LATENT = 512
ROPE = 64
TOP = 8
TOK_DEV = 64
CACHE = 512
EXPERTS = 16
CAP = 40
TOKENS = 2048
REQUESTS = 32
N_EXPERT = 16
N_DP = 2


def draw_latent_cache(key, part):
    key = jax.random.fold_in(key, 11)
    shape = (REQUESTS, CACHE, LATENT + ROPE)
    values = jnp.clip(jax.random.normal(key, shape, jnp.float32), -4.0, 4.0)
    return values.astype(jnp.bfloat16)


def draw_cache_len(key, part):
    key = jax.random.fold_in(key, 13)
    length_key, order_key = jax.random.split(key)
    drawn_lengths = jax.random.randint(length_key, (REQUESTS,), CACHE // 4, CACHE - 1)
    shuffled = jax.random.permutation(order_key, REQUESTS)
    drawn_lengths = drawn_lengths.at[shuffled[0]].set(CACHE - 2).at[shuffled[1]].set(CACHE // 4)
    return drawn_lengths.astype(jnp.int32)


def draw_queries(key, part):
    key = jax.random.fold_in(key, 17)
    shape = (REQUESTS, 2, HEADS, LATENT + ROPE)
    values = jnp.clip(jax.random.normal(key, shape, jnp.float32), -4.0, 4.0)
    return values.astype(jnp.bfloat16)


def block_scale(rng, dims, cuts, least, high):
    def one(position, parts):
        steps = jax.random.uniform(jax.random.fold_in(jax.random.fold_in(rng, 6), position), (parts,), jnp.float32, least / len(cuts), high / len(cuts))
        return jnp.repeat(jnp.exp(steps), dims[position] // parts).reshape((-1,) + (1,) * (len(dims) - position - 1))

    loudness = one(*cuts[0])
    for cut in cuts[1:]:
        loudness = loudness * one(*cut)
    return loudness


def assign_block(own_key, own, number, rows, amount, top, bound, lean):
    ranking = jax.random.permutation(own_key, amount)
    heavy_load, ordinary = shares(amount, rows * top, bound, lean, True), shares(amount, rows * top, bound, lean, False)
    places = jnp.arange(amount)

    def named(lengths, turn):
        used = int((lengths > 0).sum())
        fixed = max(1, used // 4)
        passed = fixed + (places - fixed + turn * (used - fixed)) % max(1, amount - fixed)
        return jnp.zeros((amount,), jnp.int32).at[ranking[jnp.where(places < fixed, places, passed)]].set(jnp.asarray(lengths, jnp.int32))

    lengths = jnp.where(number % 4 == 0, named(heavy_load, number // 4), named(ordinary, number - number // 4 - 1))
    mixed = jax.random.permutation(jax.random.fold_in(own, 3), amount)
    source_of, receiver = mixed[0:amount // 2 * 2:2], mixed[1:amount // 2 * 2:2]
    slack = jnp.minimum(lengths[source_of] - 1, bound - lengths[receiver]) // 2
    slack = jnp.where((source_of == ranking[0]) | (receiver == ranking[0]) | (lengths[receiver] == 0), 0, jnp.maximum(slack, 0))
    passed = jax.random.randint(jax.random.fold_in(own, 4), (amount // 2,), 0, 1 << 20) % (slack + 1)
    lengths = lengths.at[source_of].add(-passed).at[receiver].add(passed)
    labels = jnp.searchsorted(jnp.cumsum(lengths), jnp.arange(rows * top), side="right").astype(jnp.int32)
    listing = labels.reshape(top, rows).T
    listing = listing[jax.random.permutation(jax.random.fold_in(own, 1), rows)]
    turn = jax.random.randint(jax.random.fold_in(own, 2), (rows, 1), 0, top)
    return jnp.take_along_axis(listing, (jnp.arange(top)[None, :] + turn) % top, axis=1)


def shares(number_of, total, most, lean, full):
    portions = [(1 << 20) // math.isqrt(grade ** lean) + 1 for grade in range(1, number_of + 1)]
    largest = most if full else min(most, max(-(-total // number_of), total * portions[0] // sum(portions)))
    least = 1 if total - largest >= number_of - 1 else 0
    given, surplus = [largest] + [least] * (number_of - 1), total - largest - least * (number_of - 1)
    while surplus > 0:
        movable = [i for i in range(1, number_of) if given[i] < largest] or [i for i in range(1, number_of) if given[i] < most]
        pool, budget = sum([portions[i] for i in movable]), surplus
        for i in movable:
            more = min(most - given[i], max(1, budget * portions[i] // pool), surplus)
            given[i] = given[i] + more
            surplus = surplus - more
    return np.array(given)


def noise(own_key, extent, scale, limit, shards=(), kind=jnp.bfloat16):
    entries = scale * jax.random.normal(own_key, extent, jnp.float32)
    if shards:
        entries = entries * block_scale(own_key, extent, shards, -0.22, 0.18)
    return jnp.clip(entries, -limit, limit).astype(kind)


def setup_inputs(seed: int = 0, part: int = 0) -> dict:
    arg_keys = jax.random.split(jax.random.key(seed), 10)
    part_splits = jax.random.split(jax.random.fold_in(arg_keys[9], part), 10)
    tokens = noise(part_splits[0], (TOKENS, D), 1.0, 6.0, ((0, 32),))
    router_logits = noise(part_splits[1], (TOKENS, TOP), 1.5, 6.0, ((0, 32),), jnp.float32)
    expert_ids_keys = jax.random.split(jax.random.fold_in(part_splits[2], 1), TOKENS // TOK_DEV)
    expert_ids_turns = jax.random.permutation(jax.random.fold_in(part_splits[2], 3), TOKENS // TOK_DEV)
    expert_ids = jax.vmap(lambda own, number: assign_block(jax.random.fold_in(part_splits[2], 2), own, number, TOK_DEV, EXPERTS, TOP, CAP, 2))(expert_ids_keys, expert_ids_turns).reshape((TOKENS, TOP))
    gate_up = noise(arg_keys[3], (EXPERTS, 2, D, FF), D ** -0.5, 0.09375, ((0, 16), (3, 2)))
    down_proj = noise(arg_keys[4], (EXPERTS, FF, D), FF ** -0.5, 0.1875, ((0, 16), (1, 2)))
    latent_cache = draw_latent_cache(jax.random.fold_in(jax.random.fold_in(arg_keys[9], part), 71), part)
    cache_len = draw_cache_len(jax.random.fold_in(jax.random.fold_in(arg_keys[9], part), 71), part)
    new_latent = noise(part_splits[7], (REQUESTS, 2, LATENT + ROPE), 1.0, 4.0, ((0, 32),))
    queries = draw_queries(jax.random.fold_in(jax.random.fold_in(arg_keys[9], part), 71), part)
    return {"tokens": tokens, "router_logits": router_logits, "expert_ids": expert_ids, "gate_up": gate_up, "down_proj": down_proj, "latent_cache": latent_cache, "cache_len": cache_len, "new_latent": new_latent, "queries": queries}


softmax_scale = 192.0 ** -0.5
route_scale = 2.5
excluded = -1e30


def routing_gates(router_logits):
    affinity = jax.nn.sigmoid(router_logits)
    return route_scale * affinity / jnp.sum(affinity, axis=1, keepdims=True)


def expert_rows(routed_rows, gate_up_one, down_one):
    gate_part = jnp.dot(routed_rows, gate_up_one[0], preferred_element_type=jnp.float32)
    up_part = jnp.dot(routed_rows, gate_up_one[1], preferred_element_type=jnp.float32)
    hidden = (jax.nn.silu(gate_part) * up_part).astype(jnp.bfloat16)
    return jnp.dot(hidden, down_one, preferred_element_type=jnp.float32).astype(jnp.bfloat16)


def latent_attention(latent_cache, cache_len, new_latent, queries):
    key_rows = jnp.concatenate([latent_cache, new_latent], axis=1).astype(jnp.float32)
    scores = jnp.einsum("rshc,rjc->rshj", queries.astype(jnp.float32), key_rows) * softmax_scale
    cache_rows = latent_cache.shape[1]
    column = jnp.arange(cache_rows + 2, dtype=jnp.int32)
    step_ids = jnp.arange(2, dtype=jnp.int32)
    visible = (column[None, None, :] < cache_len[:, None, None]) | (column[None, None, :] == cache_rows)
    visible = visible | ((column[None, None, :] == cache_rows + 1) & (step_ids[None, :, None] == 1))
    scores = jnp.where(visible[:, :, None, :], scores, excluded)
    row_max = jnp.max(scores, axis=-1, keepdims=True)
    exp_scores = jnp.exp(scores - row_max)
    weights_bf = (exp_scores / jnp.sum(exp_scores, axis=-1, keepdims=True)).astype(jnp.bfloat16)
    context = jnp.einsum("rshj,rjc->rshc", weights_bf.astype(jnp.float32), key_rows[:, :, :LATENT])
    return context.astype(jnp.bfloat16)


def reference(tokens, router_logits, expert_ids, gate_up, down_proj, latent_cache, cache_len, new_latent, queries):
    gates = routing_gates(router_logits)
    most_rows = N_EXPERT * N_DP * CAP

    def one_expert(accumulated, expert):
        chosen = expert_ids == expert
        gate_sum = jnp.sum(jnp.where(chosen, gates, jnp.zeros_like(gates)), axis=1)
        routed = jnp.any(chosen, axis=1)
        row_index = jnp.nonzero(routed, size=most_rows, fill_value=0)[0].astype(jnp.int32)
        in_use = jnp.arange(most_rows, dtype=jnp.int32) < jnp.sum(routed.astype(jnp.int32))
        routed_rows = tokens[row_index]
        result = expert_rows(routed_rows, gate_up[expert], down_proj[expert]).astype(jnp.float32)
        weighted = jnp.where(in_use[:, None], gate_sum[row_index][:, None] * result, jnp.zeros_like(result))
        return accumulated.at[row_index].add(weighted), None

    accumulated, _ = lax.scan(one_expert, jnp.zeros(tokens.shape, jnp.float32), jnp.arange(EXPERTS, dtype=jnp.int32))
    mixed_tokens = accumulated.astype(jnp.bfloat16)
    context = latent_attention(latent_cache, cache_len, new_latent, queries)
    return mixed_tokens, context
```

```python
import jax
import jax.numpy as jnp
from jax import lax
from jax.experimental import pallas as pl
from jax.experimental.pallas import tpu as pltpu
from jax.sharding import PartitionSpec as P

LATENT = 512


softmax_scale = 192.0 ** (-0.5)
route_scale = 2.5
excluded = -1e30


def routing_gates(router_logits):
    affinity = jax.nn.sigmoid(router_logits)
    return route_scale * affinity / jnp.sum(affinity, axis=1, keepdims=True)


def hidden_units(row_block, gate_up_half):
    gate_and_up = jnp.einsum(
        "rd,gdf->rgf", row_block, gate_up_half, preferred_element_type=jnp.float32
    )
    return (jax.nn.silu(gate_and_up[:, 0]) * gate_and_up[:, 1]).astype(jnp.bfloat16)


def latent_attention(latent_cache, cache_len, new_latent, queries):
    key_rows = jnp.concatenate([latent_cache, new_latent], axis=1)
    scores = (
        jnp.einsum("rshc,rjc->rshj", queries, key_rows, preferred_element_type=jnp.float32)
        * softmax_scale
    )
    cache_rows = latent_cache.shape[1]
    column = jnp.arange(cache_rows + 2, dtype=jnp.int32)
    step_ids = jnp.arange(2, dtype=jnp.int32)
    visible = (column[None, None, :] < cache_len[:, None, None]) | (
        column[None, None, :] == cache_rows
    )
    visible = visible | (column[None, None, :] == cache_rows + 1) & (step_ids[None, :, None] == 1)
    scores = jnp.where(visible[:, :, None, :], scores, excluded)
    row_max = jnp.max(scores, axis=-1, keepdims=True)
    exp_scores = jnp.exp(scores - row_max)
    weights_bf = (exp_scores / jnp.sum(exp_scores, axis=-1, keepdims=True)).astype(jnp.bfloat16)
    context = jnp.einsum(
        "rshj,rjc->rshc", weights_bf, key_rows[:, :, :LATENT], preferred_element_type=jnp.float32
    )
    return context.astype(jnp.bfloat16)


def local(
    tokens,
    router_logits,
    expert_ids,
    gate_up,
    down_proj,
    latent_cache,
    cache_len,
    new_latent,
    queries,
):
    experts = lax.axis_size("expert")
    tok_count, top_slots = expert_ids.shape
    model_width = tokens.shape[1]
    capacity = min(tok_count, max(2, tok_count * top_slots * 5 // (4 * experts)))
    slot_count = experts * capacity
    flat_ids = expert_ids.reshape(-1)
    onehot = (flat_ids[:, None] == jnp.arange(experts, dtype=jnp.int32)[None, :]).astype(jnp.int32)
    earlier = jnp.cumsum(onehot, axis=0) - onehot
    position = jnp.sum(earlier * onehot, axis=1)
    slot_index = flat_ids * capacity + position
    placed = slot_index[None, :] == jnp.arange(slot_count, dtype=jnp.int32)[:, None]
    chooser = jnp.any(placed.reshape(slot_count, tok_count, top_slots), axis=2).astype(jnp.bfloat16)
    outgoing = jnp.dot(chooser, tokens, preferred_element_type=jnp.float32).astype(jnp.bfloat16)
    arrived = lax.all_to_all(
        outgoing.reshape(experts, capacity, model_width),
        "expert",
        split_axis=0,
        concat_axis=0,
        tiled=True,
    )
    arrived = arrived.reshape(slot_count, model_width)
    gate_up_local = gate_up[0]
    down_local = down_proj[0]
    hidden = hidden_units(arrived, lax.all_gather(gate_up_local, "dp", axis=2, tiled=True))
    summed = jnp.dot(
        hidden,
        lax.all_gather(down_local, "dp", axis=0, tiled=True),
        preferred_element_type=jnp.float32,
    )
    returned = lax.all_to_all(
        summed.astype(jnp.bfloat16).reshape(experts, capacity, model_width),
        "expert",
        split_axis=0,
        concat_axis=0,
        tiled=True,
    )
    picked = returned.reshape(slot_count, model_width)[slot_index].reshape(
        tok_count, top_slots, model_width
    )
    gates = routing_gates(router_logits)
    mixed_tokens = jnp.sum(gates[:, :, None] * picked.astype(jnp.float32), axis=1).astype(
        jnp.bfloat16
    )
    context = latent_attention(latent_cache, cache_len, new_latent, queries)
    return (mixed_tokens, context)


AUX = 128


def partners():
    me = lax.axis_index("expert")
    x, y, z = me % 2, (me // 2) % 2, me // 4
    plane = me % 4
    x_next = me + 1 - 2 * x
    y_next = me + 2 - 4 * y
    along_z = [(z + 1 - 2 * (z % 2)) * 4 + plane, (3 - z) * 4 + plane, ((z + 2) % 4) * 4 + plane]
    return me, x_next, y_next, along_z


def attend(q_ref, cache_ref, len_ref, new_ref, ctx_ref):
    q = q_ref[...]
    rows, keys = q.shape[0], cache_ref.shape[0]
    scores = softmax_scale * lax.dot_general(
        q, cache_ref[...], (((1,), (1,)), ((), ())), preferred_element_type=jnp.float32
    )
    column = lax.broadcasted_iota(jnp.int32, (rows, keys), 1)
    scores = jnp.where(column < len_ref[0], scores, excluded)
    new = new_ref[...].astype(jnp.float32)
    qf = q.astype(jnp.float32)
    first = softmax_scale * jnp.sum(qf * new[0:1], axis=1, keepdims=True)
    second = softmax_scale * jnp.sum(qf * new[1:2], axis=1, keepdims=True)
    row = lax.broadcasted_iota(jnp.int32, (rows, 1), 0)
    second = jnp.where(row >= rows // 2, second, excluded)
    top = jnp.maximum(jnp.max(scores, axis=1, keepdims=True), jnp.maximum(first, second))
    e, e1, e2 = jnp.exp(scores - top), jnp.exp(first - top), jnp.exp(second - top)
    total = jnp.sum(e, axis=1, keepdims=True) + e1 + e2
    p = (e / total).astype(jnp.bfloat16)
    p1 = (e1 / total).astype(jnp.bfloat16).astype(jnp.float32)
    p2 = (e2 / total).astype(jnp.bfloat16).astype(jnp.float32)
    ctx = jnp.dot(p, cache_ref[:, :LATENT], preferred_element_type=jnp.float32)
    ctx = ctx + p1 * new[0:1, :LATENT] + p2 * new[1:2, :LATENT]
    ctx_ref[...] = ctx.astype(ctx_ref.dtype)


def layer_kernel(
    tok_ref, log_ref, ids_ref, gu_ref, dn_ref, cache_ref, len_ref, new_ref, q_ref,
    out_ref, ctx_ref,
    xs, gu, dn, hid, part, r1x, r1y, r2x, r2y, r3,
    send_sem, recv_sem, local_sem,
):
    group, core = lax.axis_index("groups"), lax.axis_index("dp")
    me, x_next, y_next, along_z = partners()
    rows, width = tok_ref.shape
    half = rows // 2
    ffh = gu_ref.shape[2]
    mine = lambda e: (group, e, core)
    x_dev, y_dev = mine(x_next), mine(y_next)
    z_dev = [None] + [mine(e) for e in along_z]
    core_dev = (group, me, 1 - core)
    count = [0]
    sent = []

    def send(src, dst, dev):
        k = count[0]
        count[0] += 1
        copy = pltpu.make_async_remote_copy(
            src_ref=src, dst_ref=dst, send_sem=send_sem.at[k], recv_sem=recv_sem.at[k],
            device_id=dev, device_id_type=pl.DeviceIdType.MESH,
        )
        copy.start()
        sent.append(copy)
        return copy

    load = pltpu.make_async_copy(tok_ref, xs.at[0, pl.ds(0, rows), pl.ds(0, width)], local_sem.at[0])
    load.start()
    own_gu = pltpu.make_async_copy(gu_ref, gu.at[0], local_sem.at[1])
    own_dn = pltpu.make_async_copy(dn_ref, dn.at[pl.ds(0, ffh)], local_sem.at[2])

    barrier = pltpu.get_barrier_semaphore()
    greet = [x_dev, y_dev, z_dev[1], z_dev[2], z_dev[3], core_dev]
    for dev in greet:
        pl.semaphore_signal(barrier, inc=1, device_id=dev, device_id_type=pl.DeviceIdType.MESH)

    experts = lax.axis_size("expert")
    affinity = jax.nn.sigmoid(log_ref[...])
    gates = route_scale * affinity / jnp.sum(affinity, axis=1, keepdims=True)
    ids = ids_ref[...]
    lane = lax.broadcasted_iota(jnp.int32, (rows, AUX), 1)
    named = jnp.where(lane < experts, lane, lane - experts)
    weight = jnp.zeros((rows, AUX), jnp.float32)
    for k in range(ids.shape[1]):
        weight = weight + jnp.where(ids[:, k : k + 1] == named, gates[:, k : k + 1], 0.0)
    high = weight.astype(jnp.bfloat16).astype(jnp.float32)
    packed = jnp.where(lane < experts, high, jnp.where(lane < 2 * experts, weight - high, 0.0))
    xs[0, pl.ds(0, rows), pl.ds(width, AUX)] = packed.astype(jnp.bfloat16)

    pl.semaphore_wait(barrier, len(greet))
    load.wait()

    def block(i, g, lo=0, size=None):
        return xs.at[i, pl.ds(g * rows + lo, rows if size is None else size)]

    def piece(i, g, lo=0, size=None):
        return part.at[i, pl.ds(g * rows + lo, rows if size is None else size)]

    gx, gy, gz, fx, fy = {}, {}, {}, {}, {}
    gx[0] = send(block(0, 0), block(0, 1), x_dev)
    gy[0] = send(block(0, 0), block(0, 2), y_dev)
    for i in (1, 2, 3):
        gz[i] = send(block(0, 0), block(i, 0), z_dev[i])
    peer_gu = send(gu_ref, gu.at[1], core_dev)
    peer_dn = send(dn_ref, dn.at[pl.ds(ffh, ffh)], core_dev)
    own_gu.start()
    own_dn.start()

    attend(q_ref, cache_ref, len_ref, new_ref, ctx_ref)

    def forward(i):
        gx[i].wait_recv()
        fy[i] = send(block(i, 1, 0, half), block(i, 3, 0, half), y_dev)
        gy[i].wait_recv()
        fx[i] = send(block(i, 2, half, half), block(i, 3, half, half), x_dev)

    def spread(i):
        gz[i].wait_recv()
        gx[i] = send(block(i, 0), block(i, 1), x_dev)
        gy[i] = send(block(i, 0), block(i, 2), y_dev)

    tile_f, tile_d = 256, 512

    def compute(i):
        fy[i].wait_recv()
        fx[i].wait_recv()
        if i == 0:
            own_gu.wait()
            own_dn.wait()
            peer_gu.wait_recv()
            peer_dn.wait_recv()
        per = ffh // tile_f

        def up(j, carry):
            c = j // per
            cols = pl.ds(pl.multiple_of((j % per) * tile_f, tile_f), tile_f)
            x = xs[i, :, pl.ds(0, width)]
            g = jnp.dot(x, gu[c, 0, :, cols], preferred_element_type=jnp.float32)
            u = jnp.dot(x, gu[c, 1, :, cols], preferred_element_type=jnp.float32)
            h = g / (1.0 + jnp.exp(-g)) * u
            hid[:, pl.ds(pl.multiple_of(j * tile_f, tile_f), tile_f)] = h.astype(jnp.bfloat16)
            return carry

        lax.fori_loop(0, 2 * per, up, 0)
        aux = xs[i, :, pl.ds(width, AUX)].astype(jnp.float32)
        lanes = lax.broadcasted_iota(jnp.int32, aux.shape, 1)
        chosen = (lanes == me) | (lanes == me + experts)
        w = jnp.sum(jnp.where(chosen, aux, 0.0), axis=1, keepdims=True)

        def down(j, carry):
            cols = pl.ds(pl.multiple_of(j * tile_d, tile_d), tile_d)
            o = jnp.dot(hid[...], dn[:, cols], preferred_element_type=jnp.float32)
            part[i, :, cols] = (o * w).astype(jnp.bfloat16)
            return carry

        lax.fori_loop(0, width // tile_d, down, 0)

    def add(ref, others, lo=0):
        total = ref[...].astype(jnp.float32)
        for other in others:
            total = total + other[...].astype(jnp.float32)
        return total.astype(jnp.bfloat16)

    d1x, d1y, d2x, d2y, d2xb, d2yb, d3 = {}, {}, {}, {}, {}, {}, {}

    def step1(i):
        d1x[i] = send(piece(i, 3, 0, half), r1x.at[i], x_dev)
        d1y[i] = send(piece(i, 3, half, half), r1y.at[i], y_dev)
        d2x[i] = send(piece(i, 1, 0, half), r2x.at[i, pl.ds(0, half)], x_dev)
        d2y[i] = send(piece(i, 2, half, half), r2y.at[i, pl.ds(half, half)], y_dev)

    def step2(i):
        d1x[i].wait_recv()
        spot = piece(i, 2, 0, half)
        spot[...] = add(spot, [r1x.at[i]])
        d2yb[i] = send(spot, r2y.at[i, pl.ds(0, half)], y_dev)
        d1y[i].wait_recv()
        spot = piece(i, 1, half, half)
        spot[...] = add(spot, [r1y.at[i]])
        d2xb[i] = send(spot, r2x.at[i, pl.ds(half, half)], x_dev)

    def step3(i):
        for d in (d2x, d2y, d2xb, d2yb):
            d[i].wait_recv()
        if i > 0:
            spot = piece(i, 0)
            spot[...] = add(spot, [r2x.at[i], r2y.at[i]])
            d3[i] = send(spot, r3.at[i - 1], z_dev[i])

    forward(0)
    spread(1)
    compute(0)
    step1(0)
    forward(1)
    spread(2)
    compute(1)
    step1(1)
    step2(0)
    forward(2)
    spread(3)
    compute(2)
    step1(2)
    step2(1)
    forward(3)
    step3(0)
    compute(3)
    step1(3)
    step2(2)
    step3(1)
    step2(3)
    step3(2)
    step3(3)
    for i in (1, 2, 3):
        d3[i].wait_recv()
    out_ref[...] = add(piece(0, 0), [r2x.at[0], r2y.at[0], r3.at[0], r3.at[1], r3.at[2]])
    for copy in sent:
        copy.wait_send()


def local_kernel(
    tokens, router_logits, expert_ids, gate_up, down_proj, latent_cache, cache_len, new_latent, queries
):
    rows, width = tokens.shape
    ffh = gate_up.shape[3]
    bf = jnp.bfloat16
    q = queries.reshape(-1, queries.shape[-1])
    vmem = pl.BlockSpec(memory_space=pltpu.VMEM)
    hbm = pl.BlockSpec(memory_space=pl.ANY)
    mixed, ctx = pl.pallas_call(
        layer_kernel,
        out_shape=(
            jax.ShapeDtypeStruct((rows, width), bf),
            jax.ShapeDtypeStruct((q.shape[0], LATENT), bf),
        ),
        in_specs=[hbm, vmem, vmem, hbm, hbm, vmem, pl.BlockSpec(memory_space=pltpu.SMEM), vmem, vmem],
        out_specs=(vmem, vmem),
        scratch_shapes=[
            pltpu.VMEM((4, 4 * rows, width + AUX), bf),
            pltpu.VMEM((2, 2, width, ffh), bf),
            pltpu.VMEM((2 * ffh, width), bf),
            pltpu.VMEM((4 * rows, 2 * ffh), bf),
            pltpu.VMEM((4, 4 * rows, width), bf),
            pltpu.VMEM((4, rows // 2, width), bf),
            pltpu.VMEM((4, rows // 2, width), bf),
            pltpu.VMEM((4, rows, width), bf),
            pltpu.VMEM((4, rows, width), bf),
            pltpu.VMEM((3, rows, width), bf),
            pltpu.SemaphoreType.DMA((64,)),
            pltpu.SemaphoreType.DMA((64,)),
            pltpu.SemaphoreType.DMA((3,)),
        ],
        compiler_params=pltpu.CompilerParams(
            collective_id=0, has_side_effects=True, vmem_limit_bytes=60 * 1024 * 1024
        ),
    )(
        tokens, router_logits, expert_ids, gate_up[0], down_proj[0], latent_cache[0], cache_len,
        new_latent[0], q,
    )
    return mixed, ctx.reshape(queries.shape[:3] + (LATENT,))


def solution(mesh):
    whole = mesh.shape["expert"] == 16 and mesh.shape["dp"] == 2
    return jax.shard_map(
        local_kernel if whole else local,
        mesh=mesh,
        in_specs=(
            P(("groups", "expert", "dp"), None),
            P(("groups", "expert", "dp"), None),
            P(("groups", "expert", "dp"), None),
            P("expert", None, None, "dp"),
            P("expert", "dp", None),
            P(("groups", "expert", "dp"), None, None),
            P(("groups", "expert", "dp")),
            P(("groups", "expert", "dp"), None, None),
            P(("groups", "expert", "dp"), None, None, None),
        ),
        out_specs=(
            P(("groups", "expert", "dp"), None),
            P(("groups", "expert", "dp"), None, None, None),
        ),
        check_vma=False,
    )
```

```python
import jax
import jax.numpy as jnp
from jax import lax
from jax.experimental import pallas as pl
from jax.experimental.pallas import tpu as pltpu
from jax.sharding import PartitionSpec as P

LATENT = 512


softmax_scale = 192.0 ** (-0.5)
route_scale = 2.5
excluded = -1e30


def routing_gates(router_logits):
    affinity = jax.nn.sigmoid(router_logits)
    return route_scale * affinity / jnp.sum(affinity, axis=1, keepdims=True)


def hidden_units(row_block, gate_up_half):
    gate_and_up = jnp.einsum(
        "rd,gdf->rgf", row_block, gate_up_half, preferred_element_type=jnp.float32
    )
    return (jax.nn.silu(gate_and_up[:, 0]) * gate_and_up[:, 1]).astype(jnp.bfloat16)


def latent_attention(latent_cache, cache_len, new_latent, queries):
    key_rows = jnp.concatenate([latent_cache, new_latent], axis=1)
    scores = (
        jnp.einsum("rshc,rjc->rshj", queries, key_rows, preferred_element_type=jnp.float32)
        * softmax_scale
    )
    cache_rows = latent_cache.shape[1]
    column = jnp.arange(cache_rows + 2, dtype=jnp.int32)
    step_ids = jnp.arange(2, dtype=jnp.int32)
    visible = (column[None, None, :] < cache_len[:, None, None]) | (
        column[None, None, :] == cache_rows
    )
    visible = visible | (column[None, None, :] == cache_rows + 1) & (step_ids[None, :, None] == 1)
    scores = jnp.where(visible[:, :, None, :], scores, excluded)
    row_max = jnp.max(scores, axis=-1, keepdims=True)
    exp_scores = jnp.exp(scores - row_max)
    weights_bf = (exp_scores / jnp.sum(exp_scores, axis=-1, keepdims=True)).astype(jnp.bfloat16)
    context = jnp.einsum(
        "rshj,rjc->rshc", weights_bf, key_rows[:, :, :LATENT], preferred_element_type=jnp.float32
    )
    return context.astype(jnp.bfloat16)


def local(
    tokens,
    router_logits,
    expert_ids,
    gate_up,
    down_proj,
    latent_cache,
    cache_len,
    new_latent,
    queries,
):
    experts = lax.axis_size("expert")
    tok_count, top_slots = expert_ids.shape
    model_width = tokens.shape[1]
    capacity = min(tok_count, max(2, tok_count * top_slots * 5 // (4 * experts)))
    slot_count = experts * capacity
    flat_ids = expert_ids.reshape(-1)
    onehot = (flat_ids[:, None] == jnp.arange(experts, dtype=jnp.int32)[None, :]).astype(jnp.int32)
    earlier = jnp.cumsum(onehot, axis=0) - onehot
    position = jnp.sum(earlier * onehot, axis=1)
    slot_index = flat_ids * capacity + position
    placed = slot_index[None, :] == jnp.arange(slot_count, dtype=jnp.int32)[:, None]
    chooser = jnp.any(placed.reshape(slot_count, tok_count, top_slots), axis=2).astype(jnp.bfloat16)
    outgoing = jnp.dot(chooser, tokens, preferred_element_type=jnp.float32).astype(jnp.bfloat16)
    arrived = lax.all_to_all(
        outgoing.reshape(experts, capacity, model_width),
        "expert",
        split_axis=0,
        concat_axis=0,
        tiled=True,
    )
    arrived = arrived.reshape(slot_count, model_width)
    gate_up_local = gate_up[0]
    down_local = down_proj[0]
    hidden = hidden_units(arrived, lax.all_gather(gate_up_local, "dp", axis=2, tiled=True))
    summed = jnp.dot(
        hidden,
        lax.all_gather(down_local, "dp", axis=0, tiled=True),
        preferred_element_type=jnp.float32,
    )
    returned = lax.all_to_all(
        summed.astype(jnp.bfloat16).reshape(experts, capacity, model_width),
        "expert",
        split_axis=0,
        concat_axis=0,
        tiled=True,
    )
    picked = returned.reshape(slot_count, model_width)[slot_index].reshape(
        tok_count, top_slots, model_width
    )
    gates = routing_gates(router_logits)
    mixed_tokens = jnp.sum(gates[:, :, None] * picked.astype(jnp.float32), axis=1).astype(
        jnp.bfloat16
    )
    context = latent_attention(latent_cache, cache_len, new_latent, queries)
    return (mixed_tokens, context)


AUX = 128


def partners():
    me = lax.axis_index("expert")
    x, y, z = me % 2, (me // 2) % 2, me // 4
    plane = me % 4
    x_next = me + 1 - 2 * x
    y_next = me + 2 - 4 * y
    inner = ((z + 1) // 2) % 2
    mirror, second = 3 - z, (z + 2) % 4
    along_z = [
        (z + 1 - 2 * (z % 2)) * 4 + plane,
        (inner * mirror + (1 - inner) * second) * 4 + plane,
        (inner * second + (1 - inner) * mirror) * 4 + plane,
    ]
    return me, x_next, y_next, along_z, inner


def attend(q_ref, cache_ref, len_ref, new_ref, ctx_ref):
    keys, heads = cache_ref.shape[1], q_ref.shape[2]
    new = new_ref[...]
    for step in range(2):
        q = q_ref[step]
        scores = softmax_scale * lax.dot_general(
            cache_ref[...], q, (((0,), (0,)), ((), ())), preferred_element_type=jnp.float32
        )
        position = lax.broadcasted_iota(jnp.int32, (keys, heads), 0)
        scores = jnp.where(position < len_ref[0], scores, excluded)
        fresh = softmax_scale * jnp.dot(new, q, preferred_element_type=jnp.float32)
        which = lax.broadcasted_iota(jnp.int32, fresh.shape, 0)
        fresh = jnp.where(which <= step, fresh, excluded)
        top = jnp.maximum(
            jnp.max(scores, axis=0, keepdims=True), jnp.max(fresh, axis=0, keepdims=True)
        )
        e, e_new = jnp.exp(scores - top), jnp.exp(fresh - top)
        total = jnp.sum(e, axis=0, keepdims=True) + jnp.sum(e_new, axis=0, keepdims=True)
        p = (e / total).astype(jnp.bfloat16)
        p_new = (e_new / total).astype(jnp.bfloat16)
        ctx = jnp.dot(cache_ref[:LATENT], p, preferred_element_type=jnp.float32).T
        ctx = ctx + lax.dot_general(
            p_new, new[:, :LATENT], (((0,), (0,)), ((), ())), preferred_element_type=jnp.float32
        )
        ctx_ref[step] = ctx.astype(ctx_ref.dtype)


def layer_kernel(
    tok_ref, log_ref, ids_ref, gu_ref, dn_ref, cache_ref, len_ref, new_ref, q_ref,
    out_ref, ctx_ref,
    xs, gu, dn, hid, part, r1x, r1y, r2x, r2y, r3,
    send_sem, recv_sem, local_sem,
):
    group, core = lax.axis_index("groups"), lax.axis_index("dp")
    me, x_next, y_next, along_z, inner = partners()
    rows, width = tok_ref.shape
    half = rows // 2
    ffh = gu_ref.shape[2]
    mine = lambda e: (group, e, core)
    x_dev, y_dev = mine(x_next), mine(y_next)
    z_dev = [None] + [mine(e) for e in along_z]
    core_dev = (group, me, 1 - core)
    count = [0]
    sent = []

    def plan(src, dst, dev, arrival=None):
        k = count[0]
        count[0] += 1
        return pltpu.make_async_remote_copy(
            src_ref=src, dst_ref=dst, send_sem=send_sem.at[k],
            recv_sem=recv_sem.at[k if arrival is None else arrival],
            device_id=dev, device_id_type=pl.DeviceIdType.MESH,
        )

    def send(src, dst, dev, arrival=None):
        copy = plan(src, dst, dev, arrival)
        copy.start()
        sent.append(copy)
        return copy

    load = pltpu.make_async_copy(tok_ref, xs.at[0, pl.ds(0, rows), pl.ds(0, width)], local_sem.at[0])
    load.start()
    own_gu = pltpu.make_async_copy(gu_ref, gu.at[0], local_sem.at[1])
    own_dn = pltpu.make_async_copy(dn_ref, dn.at[pl.ds(0, ffh)], local_sem.at[2])

    barrier = pltpu.get_barrier_semaphore()
    greet = [x_dev, y_dev, z_dev[1], z_dev[2], z_dev[3], core_dev]
    for dev in greet:
        pl.semaphore_signal(barrier, inc=1, device_id=dev, device_id_type=pl.DeviceIdType.MESH)

    experts = lax.axis_size("expert")
    affinity = jax.nn.sigmoid(log_ref[...])
    gates = route_scale * affinity / jnp.sum(affinity, axis=0, keepdims=True)
    ids = ids_ref[...]
    lane = lax.broadcasted_iota(jnp.int32, (AUX, rows), 0)
    named = jnp.where(lane < experts, lane, lane - experts)
    weight = jnp.zeros((AUX, rows), jnp.float32)
    for k in range(ids.shape[0]):
        weight = weight + jnp.where(ids[k : k + 1] == named, gates[k : k + 1], 0.0)
    high = weight.astype(jnp.bfloat16).astype(jnp.float32)
    packed = jnp.where(lane < experts, high, jnp.where(lane < 2 * experts, weight - high, 0.0))
    xs[0, pl.ds(0, rows), pl.ds(width, AUX)] = packed.T.astype(jnp.bfloat16)

    pl.semaphore_wait(barrier, len(greet))
    load.wait()

    def block(i, g, lo=0, size=None):
        return xs.at[i, pl.ds(g * rows + lo, rows if size is None else size)]

    def piece(i, g, lo=0, size=None):
        return part.at[i, pl.ds(g * rows + lo, rows if size is None else size)]

    gx, gy, fx, fy = {}, {}, {}, {}
    inside, outside = inner == 1, inner == 0
    arrivals = {1: 58, 2: 59, 3: 60}
    gx[0] = send(block(0, 0), block(0, 1), x_dev)
    gy[0] = send(block(0, 0), block(0, 2), y_dev)
    hop1 = send(block(0, 0), block(1, 0), z_dev[1], arrivals[1])
    hop2 = plan(block(0, 0), block(2, 0), z_dev[2], arrivals[2])
    on_far = plan(block(1, 0), block(3, 0), z_dev[2], arrivals[3])
    on_near = plan(block(2, 0), block(2, 0), z_dev[1], arrivals[2])
    on_last = plan(block(3, 0), block(3, 0), z_dev[1], arrivals[3])

    @pl.when(inside)
    def _():
        hop2.start()

    peer_gu = send(gu_ref, gu.at[1], core_dev)
    peer_dn = send(dn_ref, dn.at[pl.ds(ffh, ffh)], core_dev)
    own_gu.start()
    own_dn.start()

    attend(q_ref, cache_ref, len_ref, new_ref, ctx_ref)

    def forward(i):
        gx[i].wait_recv()
        fy[i] = send(block(i, 1, 0, half), block(i, 3, 0, half), y_dev)
        gy[i].wait_recv()
        fx[i] = send(block(i, 2, half, half), block(i, 3, half, half), x_dev)

    def spread(i):
        gx[i] = send(block(i, 0), block(i, 1), x_dev)
        gy[i] = send(block(i, 0), block(i, 2), y_dev)

    tile_f, tile_d = 256, 512

    def compute(i):
        fy[i].wait_recv()
        fx[i].wait_recv()
        if i == 0:
            own_gu.wait()
            own_dn.wait()
            peer_gu.wait_recv()
            peer_dn.wait_recv()
        per = ffh // tile_f

        def up(j, carry):
            c = j // per
            cols = pl.ds(pl.multiple_of((j % per) * tile_f, tile_f), tile_f)
            x = xs[i, :, pl.ds(0, width)]
            g = jnp.dot(x, gu[c, 0, :, cols], preferred_element_type=jnp.float32)
            u = jnp.dot(x, gu[c, 1, :, cols], preferred_element_type=jnp.float32)
            h = g / (1.0 + jnp.exp(-g)) * u
            hid[:, pl.ds(pl.multiple_of(j * tile_f, tile_f), tile_f)] = h.astype(jnp.bfloat16)
            return carry

        lax.fori_loop(0, 2 * per, up, 0)
        aux = xs[i, :, pl.ds(width, AUX)].astype(jnp.float32)
        lanes = lax.broadcasted_iota(jnp.int32, aux.shape, 1)
        chosen = (lanes == me) | (lanes == me + experts)
        w = jnp.sum(jnp.where(chosen, aux, 0.0), axis=1, keepdims=True)

        def down(j, carry):
            cols = pl.ds(pl.multiple_of(j * tile_d, tile_d), tile_d)
            o = jnp.dot(hid[...], dn[:, cols], preferred_element_type=jnp.float32)
            part[i, :, cols] = (o * w).astype(jnp.bfloat16)
            return carry

        lax.fori_loop(0, width // tile_d, down, 0)

    def add(ref, others, lo=0):
        total = ref[...].astype(jnp.float32)
        for other in others:
            total = total + other[...].astype(jnp.float32)
        return total.astype(jnp.bfloat16)

    d1x, d1y, d2x, d2y, d2xb, d2yb = {}, {}, {}, {}, {}, {}

    def step1(i):
        d1x[i] = send(piece(i, 3, 0, half), r1x.at[i], x_dev)
        d1y[i] = send(piece(i, 3, half, half), r1y.at[i], y_dev)
        d2x[i] = send(piece(i, 1, 0, half), r2x.at[i, pl.ds(0, half)], x_dev)
        d2y[i] = send(piece(i, 2, half, half), r2y.at[i, pl.ds(half, half)], y_dev)

    def step2(i):
        d1x[i].wait_recv()
        spot = piece(i, 2, 0, half)
        spot[...] = add(spot, [r1x.at[i]])
        d2yb[i] = send(spot, r2y.at[i, pl.ds(0, half)], y_dev)
        d1y[i].wait_recv()
        spot = piece(i, 1, half, half)
        spot[...] = add(spot, [r1y.at[i]])
        d2xb[i] = send(spot, r2x.at[i, pl.ds(half, half)], x_dev)

    def step3(i):
        for d in (d2x, d2y, d2xb, d2yb):
            d[i].wait_recv()
        if i > 0:
            spot = piece(i, 0)
            spot[...] = add(spot, [r2x.at[i], r2y.at[i]])
            slot = {1: 0, 2: 2 - inner, 3: 1 + inner}[i]
            send(spot, r3.at[slot], z_dev[i], 61 + slot)

    hop1.wait_recv()

    @pl.when(inside)
    def _():
        on_far.start()

    spread(1)
    forward(0)
    hop2.wait_recv()

    @pl.when(inside)
    def _():
        on_near.start()

    spread(2)

    @pl.when(inside)
    def _():
        on_far.wait_recv()
        on_last.start()

    compute(0)
    forward(1)

    @pl.when(outside)
    def _():
        on_last.wait_recv()

    spread(3)
    compute(1)
    forward(2)
    compute(2)
    step1(2)
    forward(3)
    step1(1)
    step2(2)
    compute(3)
    step1(3)
    step3(2)
    step2(1)
    step2(3)
    step1(0)
    step3(1)
    step3(3)
    step2(0)
    step3(0)
    for slot in range(3):
        plan(piece(0, 0), r3.at[slot], z_dev[1], 61 + slot).wait_recv()
    out_ref[...] = add(piece(0, 0), [r2x.at[0], r2y.at[0], r3.at[0], r3.at[1], r3.at[2]])
    for copy in sent:
        copy.wait_send()

    @pl.when(inside)
    def _():
        for copy in (hop2, on_far, on_near, on_last):
            copy.wait_send()


def local_kernel(
    tokens, router_logits, expert_ids, gate_up, down_proj, latent_cache, cache_len, new_latent, queries
):
    rows, width = tokens.shape
    ffh = gate_up.shape[3]
    bf = jnp.bfloat16
    q = queries[0].swapaxes(1, 2)
    vmem = pl.BlockSpec(memory_space=pltpu.VMEM)
    hbm = pl.BlockSpec(memory_space=pl.ANY)
    mixed, ctx = pl.pallas_call(
        layer_kernel,
        out_shape=(
            jax.ShapeDtypeStruct((rows, width), bf),
            jax.ShapeDtypeStruct(queries.shape[1:3] + (LATENT,), bf),
        ),
        in_specs=[hbm, vmem, vmem, hbm, hbm, vmem, pl.BlockSpec(memory_space=pltpu.SMEM), vmem, vmem],
        out_specs=(vmem, vmem),
        scratch_shapes=[
            pltpu.VMEM((4, 4 * rows, width + AUX), bf),
            pltpu.VMEM((2, 2, width, ffh), bf),
            pltpu.VMEM((2 * ffh, width), bf),
            pltpu.VMEM((4 * rows, 2 * ffh), bf),
            pltpu.VMEM((4, 4 * rows, width), bf),
            pltpu.VMEM((4, rows // 2, width), bf),
            pltpu.VMEM((4, rows // 2, width), bf),
            pltpu.VMEM((4, rows, width), bf),
            pltpu.VMEM((4, rows, width), bf),
            pltpu.VMEM((3, rows, width), bf),
            pltpu.SemaphoreType.DMA((64,)),
            pltpu.SemaphoreType.DMA((64,)),
            pltpu.SemaphoreType.DMA((3,)),
        ],
        compiler_params=pltpu.CompilerParams(
            collective_id=0, has_side_effects=True, vmem_limit_bytes=60 * 1024 * 1024
        ),
    )(
        tokens, router_logits.T, expert_ids.T, gate_up[0], down_proj[0], latent_cache[0].T, cache_len,
        new_latent[0], q,
    )
    return mixed, ctx[None]


def solution(mesh):
    whole = mesh.shape["expert"] == 16 and mesh.shape["dp"] == 2
    return jax.shard_map(
        local_kernel if whole else local,
        mesh=mesh,
        in_specs=(
            P(("groups", "expert", "dp"), None),
            P(("groups", "expert", "dp"), None),
            P(("groups", "expert", "dp"), None),
            P("expert", None, None, "dp"),
            P("expert", "dp", None),
            P(("groups", "expert", "dp"), None, None),
            P(("groups", "expert", "dp")),
            P(("groups", "expert", "dp"), None, None),
            P(("groups", "expert", "dp"), None, None, None),
        ),
        out_specs=(
            P(("groups", "expert", "dp"), None),
            P(("groups", "expert", "dp"), None, None, None),
        ),
        check_vma=False,
    )
```

```python
import jax
import jax.numpy as jnp
from jax import lax
from jax.experimental import pallas as pl
from jax.experimental.pallas import tpu as pltpu
from jax.sharding import PartitionSpec as P

LATENT = 512


softmax_scale = 192.0 ** (-0.5)
route_scale = 2.5
excluded = -1e30


def routing_gates(router_logits):
    affinity = jax.nn.sigmoid(router_logits)
    return route_scale * affinity / jnp.sum(affinity, axis=1, keepdims=True)


def hidden_units(row_block, gate_up_half):
    gate_and_up = jnp.einsum(
        "rd,gdf->rgf", row_block, gate_up_half, preferred_element_type=jnp.float32
    )
    return (jax.nn.silu(gate_and_up[:, 0]) * gate_and_up[:, 1]).astype(jnp.bfloat16)


def latent_attention(latent_cache, cache_len, new_latent, queries):
    key_rows = jnp.concatenate([latent_cache, new_latent], axis=1)
    scores = (
        jnp.einsum("rshc,rjc->rshj", queries, key_rows, preferred_element_type=jnp.float32)
        * softmax_scale
    )
    cache_rows = latent_cache.shape[1]
    column = jnp.arange(cache_rows + 2, dtype=jnp.int32)
    step_ids = jnp.arange(2, dtype=jnp.int32)
    visible = (column[None, None, :] < cache_len[:, None, None]) | (
        column[None, None, :] == cache_rows
    )
    visible = visible | (column[None, None, :] == cache_rows + 1) & (step_ids[None, :, None] == 1)
    scores = jnp.where(visible[:, :, None, :], scores, excluded)
    row_max = jnp.max(scores, axis=-1, keepdims=True)
    exp_scores = jnp.exp(scores - row_max)
    weights_bf = (exp_scores / jnp.sum(exp_scores, axis=-1, keepdims=True)).astype(jnp.bfloat16)
    context = jnp.einsum(
        "rshj,rjc->rshc", weights_bf, key_rows[:, :, :LATENT], preferred_element_type=jnp.float32
    )
    return context.astype(jnp.bfloat16)


def local(
    tokens,
    router_logits,
    expert_ids,
    gate_up,
    down_proj,
    latent_cache,
    cache_len,
    new_latent,
    queries,
):
    experts = lax.axis_size("expert")
    tok_count, top_slots = expert_ids.shape
    model_width = tokens.shape[1]
    capacity = min(tok_count, max(2, tok_count * top_slots * 5 // (4 * experts)))
    slot_count = experts * capacity
    flat_ids = expert_ids.reshape(-1)
    onehot = (flat_ids[:, None] == jnp.arange(experts, dtype=jnp.int32)[None, :]).astype(jnp.int32)
    earlier = jnp.cumsum(onehot, axis=0) - onehot
    position = jnp.sum(earlier * onehot, axis=1)
    slot_index = flat_ids * capacity + position
    placed = slot_index[None, :] == jnp.arange(slot_count, dtype=jnp.int32)[:, None]
    chooser = jnp.any(placed.reshape(slot_count, tok_count, top_slots), axis=2).astype(jnp.bfloat16)
    outgoing = jnp.dot(chooser, tokens, preferred_element_type=jnp.float32).astype(jnp.bfloat16)
    arrived = lax.all_to_all(
        outgoing.reshape(experts, capacity, model_width),
        "expert",
        split_axis=0,
        concat_axis=0,
        tiled=True,
    )
    arrived = arrived.reshape(slot_count, model_width)
    gate_up_local = gate_up[0]
    down_local = down_proj[0]
    hidden = hidden_units(arrived, lax.all_gather(gate_up_local, "dp", axis=2, tiled=True))
    summed = jnp.dot(
        hidden,
        lax.all_gather(down_local, "dp", axis=0, tiled=True),
        preferred_element_type=jnp.float32,
    )
    returned = lax.all_to_all(
        summed.astype(jnp.bfloat16).reshape(experts, capacity, model_width),
        "expert",
        split_axis=0,
        concat_axis=0,
        tiled=True,
    )
    picked = returned.reshape(slot_count, model_width)[slot_index].reshape(
        tok_count, top_slots, model_width
    )
    gates = routing_gates(router_logits)
    mixed_tokens = jnp.sum(gates[:, :, None] * picked.astype(jnp.float32), axis=1).astype(
        jnp.bfloat16
    )
    context = latent_attention(latent_cache, cache_len, new_latent, queries)
    return (mixed_tokens, context)


AUX = 128


def partners():
    me = lax.axis_index("expert")
    x, y, z = me % 2, (me // 2) % 2, me // 4
    plane = me % 4
    x_next = me + 1 - 2 * x
    y_next = me + 2 - 4 * y
    inner = ((z + 1) // 2) % 2
    mirror, second = 3 - z, (z + 2) % 4
    along_z = [
        (z + 1 - 2 * (z % 2)) * 4 + plane,
        (inner * mirror + (1 - inner) * second) * 4 + plane,
        (inner * second + (1 - inner) * mirror) * 4 + plane,
    ]
    return me, x_next, y_next, along_z, inner


def attend(q_ref, cache_ref, len_ref, new_ref, ctx_ref):
    keys, heads = cache_ref.shape[1], q_ref.shape[2]
    new = new_ref[...]
    for step in range(2):
        q = q_ref[step]
        scores = softmax_scale * lax.dot_general(
            cache_ref[...], q, (((0,), (0,)), ((), ())), preferred_element_type=jnp.float32
        )
        position = lax.broadcasted_iota(jnp.int32, (keys, heads), 0)
        scores = jnp.where(position < len_ref[0], scores, excluded)
        fresh = softmax_scale * jnp.dot(new, q, preferred_element_type=jnp.float32)
        which = lax.broadcasted_iota(jnp.int32, fresh.shape, 0)
        fresh = jnp.where(which <= step, fresh, excluded)
        top = jnp.maximum(
            jnp.max(scores, axis=0, keepdims=True), jnp.max(fresh, axis=0, keepdims=True)
        )
        e, e_new = jnp.exp(scores - top), jnp.exp(fresh - top)
        total = jnp.sum(e, axis=0, keepdims=True) + jnp.sum(e_new, axis=0, keepdims=True)
        p = (e / total).astype(jnp.bfloat16)
        p_new = (e_new / total).astype(jnp.bfloat16)
        ctx = jnp.dot(cache_ref[:LATENT], p, preferred_element_type=jnp.float32).T
        ctx = ctx + lax.dot_general(
            p_new, new[:, :LATENT], (((0,), (0,)), ((), ())), preferred_element_type=jnp.float32
        )
        ctx_ref[step] = ctx.astype(ctx_ref.dtype)


def layer_kernel(
    tok_ref, log_ref, ids_ref, gu_ref, dn_ref, cache_ref, len_ref, new_ref, q_ref,
    out_ref, ctx_ref,
    xs, gu, dn, hid, part, r1x, r1y, r2x, r2y, r3,
    send_sem, recv_sem, local_sem,
):
    group, core = lax.axis_index("groups"), lax.axis_index("dp")
    me, x_next, y_next, along_z, inner = partners()
    rows, width = tok_ref.shape
    half = rows // 2
    ffh = gu_ref.shape[2]
    mine = lambda e: (group, e, core)
    x_dev, y_dev = mine(x_next), mine(y_next)
    z_dev = [None] + [mine(e) for e in along_z]
    core_dev = (group, me, 1 - core)
    count = [0]
    sent = []

    def plan(src, dst, dev, arrival=None):
        k = count[0]
        count[0] += 1
        return pltpu.make_async_remote_copy(
            src_ref=src, dst_ref=dst, send_sem=send_sem.at[k],
            recv_sem=recv_sem.at[k if arrival is None else arrival],
            device_id=dev, device_id_type=pl.DeviceIdType.MESH,
        )

    def send(src, dst, dev, arrival=None):
        copy = plan(src, dst, dev, arrival)
        copy.start()
        sent.append(copy)
        return copy

    load = pltpu.make_async_copy(tok_ref, xs.at[0, pl.ds(0, rows), pl.ds(0, width)], local_sem.at[0])
    load.start()
    own_gu = pltpu.make_async_copy(gu_ref, gu.at[0], local_sem.at[1])
    own_dn = pltpu.make_async_copy(dn_ref, dn.at[pl.ds(0, ffh)], local_sem.at[2])

    barrier = pltpu.get_barrier_semaphore()
    greet = [x_dev, y_dev, z_dev[1], z_dev[2], z_dev[3], core_dev]
    for dev in greet:
        pl.semaphore_signal(barrier, inc=1, device_id=dev, device_id_type=pl.DeviceIdType.MESH)

    experts = lax.axis_size("expert")
    affinity = jax.nn.sigmoid(log_ref[...])
    gates = route_scale * affinity / jnp.sum(affinity, axis=0, keepdims=True)
    ids = ids_ref[...]
    lane = lax.broadcasted_iota(jnp.int32, (AUX, rows), 0)
    named = jnp.where(lane < experts, lane, lane - experts)
    weight = jnp.zeros((AUX, rows), jnp.float32)
    for k in range(ids.shape[0]):
        weight = weight + jnp.where(ids[k : k + 1] == named, gates[k : k + 1], 0.0)
    high = weight.astype(jnp.bfloat16).astype(jnp.float32)
    packed = jnp.where(lane < experts, high, jnp.where(lane < 2 * experts, weight - high, 0.0))
    xs[0, pl.ds(0, rows), pl.ds(width, AUX)] = packed.T.astype(jnp.bfloat16)

    pl.semaphore_wait(barrier, len(greet))
    load.wait()

    def block(i, g, lo=0, size=None):
        return xs.at[i, pl.ds(g * rows + lo, rows if size is None else size)]

    def piece(i, g, lo=0, size=None):
        return part.at[i, pl.ds(g * rows + lo, rows if size is None else size)]

    gx, gy, fx, fy = {}, {}, {}, {}
    inside, outside = inner == 1, inner == 0
    arrivals = {1: 58, 2: 59, 3: 60}
    gx[0] = send(block(0, 0), block(0, 1), x_dev)
    gy[0] = send(block(0, 0), block(0, 2), y_dev)
    hop1 = send(block(0, 0), block(1, 0), z_dev[1], arrivals[1])
    hop2 = plan(block(0, 0), block(2, 0), z_dev[2], arrivals[2])
    on_far = plan(block(1, 0), block(3, 0), z_dev[2], arrivals[3])
    on_near = plan(block(2, 0), block(2, 0), z_dev[1], arrivals[2])
    on_last = plan(block(3, 0), block(3, 0), z_dev[1], arrivals[3])

    @pl.when(inside)
    def _():
        hop2.start()

    peer_gu = send(gu_ref, gu.at[1], core_dev)
    peer_dn = send(dn_ref, dn.at[pl.ds(ffh, ffh)], core_dev)
    own_gu.start()
    own_dn.start()

    attend(q_ref, cache_ref, len_ref, new_ref, ctx_ref)

    def forward(i):
        gx[i].wait_recv()
        fy[i] = send(block(i, 1, 0, half), block(i, 3, 0, half), y_dev)
        gy[i].wait_recv()
        fx[i] = send(block(i, 2, half, half), block(i, 3, half, half), x_dev)

    def spread(i):
        gx[i] = send(block(i, 0), block(i, 1), x_dev)
        gy[i] = send(block(i, 0), block(i, 2), y_dev)

    tile_f, tile_d = 256, 512

    def compute(i):
        fy[i].wait_recv()
        fx[i].wait_recv()
        if i == 0:
            own_gu.wait()
            own_dn.wait()
            peer_gu.wait_recv()
            peer_dn.wait_recv()
        per = ffh // tile_f

        def up(j, carry):
            c = j // per
            cols = pl.ds(pl.multiple_of((j % per) * tile_f, tile_f), tile_f)
            x = xs[i, :, pl.ds(0, width)]
            g = jnp.dot(x, gu[c, 0, :, cols], preferred_element_type=jnp.float32)
            u = jnp.dot(x, gu[c, 1, :, cols], preferred_element_type=jnp.float32)
            h = g / (1.0 + jnp.exp(-g)) * u
            hid[:, pl.ds(pl.multiple_of(j * tile_f, tile_f), tile_f)] = h.astype(jnp.bfloat16)
            return carry

        lax.fori_loop(0, 2 * per, up, 0)
        aux = xs[i, :, pl.ds(width, AUX)].astype(jnp.float32)
        lanes = lax.broadcasted_iota(jnp.int32, aux.shape, 1)
        chosen = (lanes == me) | (lanes == me + experts)
        w = jnp.sum(jnp.where(chosen, aux, 0.0), axis=1, keepdims=True)

        def down(j, carry):
            cols = pl.ds(pl.multiple_of(j * tile_d, tile_d), tile_d)
            o = jnp.dot(hid[...], dn[:, cols], preferred_element_type=jnp.float32)
            part[i, :, cols] = (o * w).astype(jnp.bfloat16)
            return carry

        lax.fori_loop(0, width // tile_d, down, 0)

    def add(ref, others, lo=0):
        total = ref[...].astype(jnp.float32)
        for other in others:
            total = total + other[...].astype(jnp.float32)
        return total.astype(jnp.bfloat16)

    d1x, d1y, d2x, d2y, d2xb, d2yb = {}, {}, {}, {}, {}, {}

    def step1(i):
        d1x[i] = send(piece(i, 3, 0, half), r1x.at[i], x_dev)
        d1y[i] = send(piece(i, 3, half, half), r1y.at[i], y_dev)
        d2x[i] = send(piece(i, 1, 0, half), r2x.at[i, pl.ds(0, half)], x_dev)
        d2y[i] = send(piece(i, 2, half, half), r2y.at[i, pl.ds(half, half)], y_dev)

    def step2(i):
        d1x[i].wait_recv()
        spot = piece(i, 2, 0, half)
        spot[...] = add(spot, [r1x.at[i]])
        d2yb[i] = send(spot, r2y.at[i, pl.ds(0, half)], y_dev)
        d1y[i].wait_recv()
        spot = piece(i, 1, half, half)
        spot[...] = add(spot, [r1y.at[i]])
        d2xb[i] = send(spot, r2x.at[i, pl.ds(half, half)], x_dev)

    def step3(i):
        for d in (d2x, d2y, d2xb, d2yb):
            d[i].wait_recv()
        if i > 0:
            spot = piece(i, 0)
            spot[...] = add(spot, [r2x.at[i], r2y.at[i]])
            slot = {1: 0, 2: 2 - inner, 3: 1 + inner}[i]
            send(spot, r3.at[slot], z_dev[i], 61 + slot)

    hop1.wait_recv()

    @pl.when(inside)
    def _():
        on_far.start()

    spread(1)
    forward(0)
    hop2.wait_recv()

    @pl.when(inside)
    def _():
        on_near.start()

    spread(2)

    @pl.when(inside)
    def _():
        on_far.wait_recv()
        on_last.start()

    forward(1)
    compute(0)

    @pl.when(outside)
    def _():
        on_last.wait_recv()

    spread(3)
    forward(2)
    compute(1)
    forward(3)
    compute(2)
    step1(2)
    step1(1)
    step2(2)
    compute(3)
    step1(3)
    step3(2)
    step2(1)
    step2(3)
    step1(0)
    step3(1)
    step3(3)
    step2(0)
    step3(0)
    for slot in range(3):
        plan(piece(0, 0), r3.at[slot], z_dev[1], 61 + slot).wait_recv()
    out_ref[...] = add(piece(0, 0), [r2x.at[0], r2y.at[0], r3.at[0], r3.at[1], r3.at[2]])
    for copy in sent:
        copy.wait_send()

    @pl.when(inside)
    def _():
        for copy in (hop2, on_far, on_near, on_last):
            copy.wait_send()


def local_kernel(
    tokens, router_logits, expert_ids, gate_up, down_proj, latent_cache, cache_len, new_latent, queries
):
    rows, width = tokens.shape
    ffh = gate_up.shape[3]
    bf = jnp.bfloat16
    q = queries[0].swapaxes(1, 2)
    vmem = pl.BlockSpec(memory_space=pltpu.VMEM)
    hbm = pl.BlockSpec(memory_space=pl.ANY)
    mixed, ctx = pl.pallas_call(
        layer_kernel,
        out_shape=(
            jax.ShapeDtypeStruct((rows, width), bf),
            jax.ShapeDtypeStruct(queries.shape[1:3] + (LATENT,), bf),
        ),
        in_specs=[hbm, vmem, vmem, hbm, hbm, vmem, pl.BlockSpec(memory_space=pltpu.SMEM), vmem, vmem],
        out_specs=(vmem, vmem),
        scratch_shapes=[
            pltpu.VMEM((4, 4 * rows, width + AUX), bf),
            pltpu.VMEM((2, 2, width, ffh), bf),
            pltpu.VMEM((2 * ffh, width), bf),
            pltpu.VMEM((4 * rows, 2 * ffh), bf),
            pltpu.VMEM((4, 4 * rows, width), bf),
            pltpu.VMEM((4, rows // 2, width), bf),
            pltpu.VMEM((4, rows // 2, width), bf),
            pltpu.VMEM((4, rows, width), bf),
            pltpu.VMEM((4, rows, width), bf),
            pltpu.VMEM((3, rows, width), bf),
            pltpu.SemaphoreType.DMA((64,)),
            pltpu.SemaphoreType.DMA((64,)),
            pltpu.SemaphoreType.DMA((3,)),
        ],
        compiler_params=pltpu.CompilerParams(
            collective_id=0, has_side_effects=True, vmem_limit_bytes=60 * 1024 * 1024
        ),
    )(
        tokens, router_logits.T, expert_ids.T, gate_up[0], down_proj[0], latent_cache[0].T, cache_len,
        new_latent[0], q,
    )
    return mixed, ctx[None]


def solution(mesh):
    whole = mesh.shape["expert"] == 16 and mesh.shape["dp"] == 2
    return jax.shard_map(
        local_kernel if whole else local,
        mesh=mesh,
        in_specs=(
            P(("groups", "expert", "dp"), None),
            P(("groups", "expert", "dp"), None),
            P(("groups", "expert", "dp"), None),
            P("expert", None, None, "dp"),
            P("expert", "dp", None),
            P(("groups", "expert", "dp"), None, None),
            P(("groups", "expert", "dp")),
            P(("groups", "expert", "dp"), None, None),
            P(("groups", "expert", "dp"), None, None, None),
        ),
        out_specs=(
            P(("groups", "expert", "dp"), None),
            P(("groups", "expert", "dp"), None, None, None),
        ),
        check_vma=False,
    )
```
